32 devices in a mesh: grp: 4 (over z), blk: 8 (over y, x, core).
Axes of the slice: x: 2, y: 2, z: 4, core: 2. Of those that a mesh axis runs over, the one named last changes fastest.
Arguments:
- band_states: bfloat16 [64, 8, 1152], P(('grp', 'blk')), may hold values from -6 to 6
- kpoint_ids: int32 [64], P(('grp', 'blk')), may hold values from 0 to 2303, as said below
- screened: bfloat16 [2304, 1152], P('grp'), may hold values from 0.19921875 to 5
- coulomb: float32 [1152], replicated, may hold values from 0.2 to 5
- umklapp_map: int32 [4, 1152], replicated, may hold values from 0 to 1151, each once within a row
Outputs:
- kernel: float32 [64, 4, 512], P(('grp', 'blk'))
- mirror: float32 [64, 4, 512], P(('grp', 'blk'))
The draws below stay inside these ranges and needn't reach their ends.
Inputs may be any that keep to these rules, and one draw needn't show every extreme that they name: `kpoint_ids`: 64 distinct flat indices row * 48 + col of the 48 x 48 grid, in increasing order along the k-points. `umklapp_map`: each row is a permutation of the 1152 G-vector indices.
All inputs are finite; a program needn't handle non-finite values.
Results may differ from the reference program's by a relative error of at most 0.011.
Values may be sent and summed in bfloat16 or wider, within the bound.
A program may use at most 128 MiB of HBM per device.

```python
import math
import jax
import jax.numpy as jnp
from jax import lax

NKX = 48
NKY = 48
NV = 4
NC = 4
NG = 1152
NU = 4
STEPS = 4
KD = 2
NK = 64
NQ = 2304
N_GRP = 4
N_BLK = 8


def draw_kpoint_ids(key, part):
    key = jax.random.fold_in(key, 17)
    interior = 1 + jax.random.permutation(key, NKX * NKY - 2)[:NK - 2]
    extremes = jnp.array([0, NKX * NKY - 1], dtype=jnp.int32)
    chosen = jnp.concatenate([extremes, interior.astype(jnp.int32)])
    return jnp.sort(chosen)


def block_scale(own_key, shape, shards, smallest, largest):
    factor_of = 1.0
    for dim, parts in shards:
        draws = jax.random.uniform(jax.random.fold_in(jax.random.fold_in(own_key, 6), dim), (parts,), jnp.float32, smallest / len(shards), largest / len(shards))
        factor_of = factor_of * jnp.repeat(jnp.exp(draws), shape[dim] // parts).reshape((-1,) + (1,) * (len(shape) - 1 - dim))
    return factor_of


def bell_draw(key, dims, deviation, limit, pieces=(), kind=jnp.bfloat16):
    values = deviation * jax.random.normal(key, dims, jnp.float32)
    if pieces:
        values = values * block_scale(key, dims, pieces, -0.22, 0.18)
    return jnp.clip(values, -limit, limit).astype(kind)


def setup_inputs(seed: int = 0) -> dict:
    keys = jax.random.split(jax.random.key(seed), 6)
    band_states = bell_draw(keys[0], (NK, NV + NC, NG), 1.0, 6.0, ((0, 32),))
    kpoint_ids = draw_kpoint_ids(jax.random.fold_in(keys[5], 71), 0)
    screened = jnp.clip(jnp.exp(math.log(5.0) - 3.2227897 * jax.random.uniform(keys[2], (NQ, NG), jnp.float32) ** block_scale(keys[2], (NQ, NG), ((0, 4),), -0.2, 0.2)), 0.19921875, 5.0).astype(jnp.bfloat16)
    coulomb = jnp.clip(jnp.exp(jax.random.uniform(keys[3], (NG,), jnp.float32, math.log(0.2), math.log(5.0))), 0.2, 5.0)
    umklapp_map = jax.vmap(lambda own: jax.random.permutation(own, NG))(jax.random.split(keys[4], NU)).reshape((NU, NG)).astype(jnp.int32)
    return dict(band_states=band_states, kpoint_ids=kpoint_ids, screened=screened, coulomb=coulomb, umklapp_map=umklapp_map)


def plane_table(points):
    indices = jnp.arange(points, dtype=jnp.int32)
    phase_index = (2 * indices[:, None] + 1) * (2 * indices[None, :] + 1) % (8 * points)
    angles = phase_index.astype(jnp.float32) * (math.pi / (4 * points))
    return (jnp.cos(angles) * math.sqrt(2.0 / points)).astype(jnp.bfloat16)

def cross_products(first_set, second_set):
    product_values = first_set.astype(jnp.float32)[:, None, :, None, :] * second_set.astype(jnp.float32)[None, :, None, :, :]
    merged = product_values.reshape(first_set.shape[0], second_set.shape[0], first_set.shape[1] * second_set.shape[1], first_set.shape[2])
    return merged.astype(jnp.bfloat16)

def same_products(valence, conduction):
    product_values = valence.astype(jnp.float32)[:, :, None, :] * conduction.astype(jnp.float32)[:, None, :, :]
    merged = product_values.reshape(valence.shape[0], valence.shape[1] * conduction.shape[1], valence.shape[2])
    return merged.astype(jnp.bfloat16)

def project(products, planes):
    array_shape = products.shape
    flattened = products.reshape(-1, array_shape[-1]).astype(jnp.float32)
    result = jnp.dot(flattened, planes.astype(jnp.float32), preferred_element_type=jnp.float32)
    return result.astype(jnp.bfloat16).reshape(array_shape)

def grid_terms(own_ids, other_ids):
    own_row = own_ids // NKY
    own_col = own_ids % NKY
    other_row = other_ids // NKY
    other_col = other_ids % NKY
    momentum = (own_row[:, None] - other_row[None, :]) % NKX * NKY + (own_col[:, None] - other_col[None, :]) % NKY
    shift_class = (own_row[:, None] < other_row[None, :]).astype(jnp.int32) + 2 * (own_col[:, None] < other_col[None, :]).astype(jnp.int32)
    return (momentum.astype(jnp.int32), shift_class)

def kernel_pair(conduction, valence, partner_states, screening, weighted_x, partner_pairs, planes):
    own_count = conduction.shape[0]
    other_count = partner_states.shape[0]
    points = conduction.shape[2]
    cond_products = cross_products(conduction, partner_states[:, NV:])
    val_products = cross_products(valence, partner_states[:, :NV])
    stacked = jnp.concatenate([cond_products, val_products], axis=2)
    densities = project(stacked, planes)
    cond_rho = densities[:, :, :NC * NC]
    val_rho = densities[:, :, NC * NC:]
    weighted = (cond_rho.astype(jnp.float32) * screening[:, :, None, :].astype(jnp.float32)).astype(jnp.bfloat16)
    direct = jnp.einsum('kjag,kjbg->kjba', weighted.astype(jnp.float32), val_rho.astype(jnp.float32))
    direct = direct.reshape(own_count, other_count, NV, NV, NC, NC).transpose(0, 1, 2, 4, 3, 5)
    exchange = jnp.einsum('kag,jbg->kjab', weighted_x.astype(jnp.float32), partner_pairs.astype(jnp.float32))
    exchange = exchange.reshape(own_count, other_count, NV, NC, NV, NC)
    return (2.0 * exchange - direct) * (1.0 / math.sqrt(points))

def reference(band_states, kpoint_ids, screened, coulomb, umklapp_map):
    points = band_states.shape[2]
    planes = plane_table(points)
    valence = band_states[:, :NV]
    conduction = band_states[:, NV:]
    own_pairs = project(same_products(valence, conduction), planes)
    weighted_x = (own_pairs.astype(jnp.float32) * coulomb).astype(jnp.bfloat16)

    def one_device(device):
        group = device // N_BLK
        position = device % N_BLK
        first_own = (device * KD).astype(jnp.int32)
        own_states = lax.dynamic_slice_in_dim(band_states, first_own, KD, 0)
        own_ids = lax.dynamic_slice_in_dim(kpoint_ids, first_own, KD, 0)
        own_x = lax.dynamic_slice_in_dim(weighted_x, first_own, KD, 0)
        kernel_rows = []
        for offset in range(1, STEPS + 1):
            source = ((group * N_BLK + (position - offset) % N_BLK) * KD).astype(jnp.int32)
            other_states = lax.dynamic_slice_in_dim(band_states, source, KD, 0)
            other_ids = lax.dynamic_slice_in_dim(kpoint_ids, source, KD, 0)
            other_pairs = lax.dynamic_slice_in_dim(own_pairs, source, KD, 0)
            momentum, shift_class = grid_terms(own_ids, other_ids)
            screening = jnp.take_along_axis(screened[momentum], umklapp_map[shift_class], axis=-1)
            kernel_block = kernel_pair(own_states[:, NV:], own_states[:, :NV], other_states, screening, own_x, other_pairs, planes)
            kernel_rows.append(kernel_block.reshape(KD, -1))
        return jnp.stack(kernel_rows, axis=1)
    devices_all = N_GRP * N_BLK
    blocks = lax.map(one_device, jnp.arange(devices_all, dtype=jnp.int32))
    total_k = devices_all * KD
    kernel = blocks.reshape(total_k, STEPS, KD * NV * NC * NV * NC)
    all_k = jnp.arange(total_k, dtype=jnp.int32)
    device_of = all_k // KD
    group_of = device_of // N_BLK
    position_of = device_of % N_BLK
    local_of = all_k % KD
    offsets = jnp.arange(1, STEPS + 1, dtype=jnp.int32)
    source_dev = group_of[:, None] * N_BLK + (position_of[:, None] + offsets[None, :]) % N_BLK
    source_k = source_dev[:, :, None] * KD + jnp.arange(KD, dtype=jnp.int32)[None, None, :]
    shaped = kernel.reshape(total_k, STEPS, KD, NV, NC, NV, NC)
    picked = shaped[source_k, jnp.arange(STEPS, dtype=jnp.int32)[None, :, None], local_of[:, None, None]]
    mirror = picked.transpose(0, 1, 2, 5, 6, 3, 4).reshape(total_k, STEPS, KD * NV * NC * NV * NC)
    return (kernel, mirror)
```

```python
import functools
import math

import jax
import jax.numpy as jnp
import ml_dtypes
import numpy as np
from jax import lax
from jax.experimental import pallas as pl
from jax.experimental.pallas import tpu as pltpu
from jax.sharding import PartitionSpec as P

NKX = 48
NKY = 48
NV = 4
NC = 4
STEPS = 4
KD = 2
NB = NV + NC
PAIRS = STEPS * KD * KD
MESH = pl.DeviceIdType.MESH
F32 = jnp.float32
BF16 = jnp.bfloat16
I32 = jnp.int32


def plane_table(points):
    indices = np.arange(points, dtype=np.int64)
    phase_index = (2 * indices[:, None] + 1) * (2 * indices[None, :] + 1) % (8 * points)
    angles = phase_index * (math.pi / (4 * points))
    return (np.cos(angles) * math.sqrt(2.0 / points)).astype(np.float32).astype(ml_dtypes.bfloat16)


def dot_nn(a, b):
    return lax.dot_general(a, b, (((1,), (0,)), ((), ())), preferred_element_type=F32)


def dot_nt(a, b):
    return lax.dot_general(a, b, (((1,), (1,)), ((), ())), preferred_element_type=F32)


def iota(shape, dim):
    return lax.broadcasted_iota(I32, shape, dim)


def split_dot(value, table):
    rows = value.shape[0]
    high = value.astype(BF16)
    low = (value - high.astype(F32)).astype(BF16)
    both = dot_nn(jnp.concatenate([high, low], axis=0), table)
    return both[:rows] + both[rows:]


def split_grid(ids):
    row = (ids * 43691) >> 21
    return row, ids - row * NKY


def kernel_body(
    n_grp, n_blk, ids_ref, band_hbm, screened_hbm, coulomb_hbm, umklapp_hbm, planes_hbm,
    out_ref, mirror_ref,
    band, screened, coulomb, umklapp, planes,
    id_send, id_recv, q_slots, w_send, w_recv, band_recv,
    products, densities, weighted, screen, shuffle_d, shuffle_e, shuffle_m, m_send, m_recv,
    local_sem, id_ss, id_rs, q_ss, q_rs, w_ss, w_rs, b_ss, b_rs, m_ss, m_rs,
):
    grp = lax.axis_index("grp")
    blk = lax.axis_index("blk")
    points = planes.shape[1]
    owned = screened.shape[0]

    locals_ = [
        pltpu.make_async_copy(src, dst, local_sem.at[n])
        for n, (src, dst) in enumerate(
            [
                (band_hbm, band),
                (screened_hbm, screened),
                (planes_hbm, planes),
                (umklapp_hbm, umklapp),
                (coulomb_hbm, coulomb),
            ]
        )
    ]
    for copy in locals_:
        copy.start()

    def blk_dev(offset):
        return (grp, lax.rem(blk + offset + n_blk, n_blk))

    def grp_dev(offset):
        return (lax.rem(grp + offset + n_grp, n_grp), blk)

    barrier = pltpu.get_barrier_semaphore()
    offsets = sorted({s % n_blk for s in range(1, STEPS + 1)} | {-s % n_blk for s in range(1, STEPS + 1)})
    for offset in offsets:
        pl.semaphore_signal(barrier, inc=1, device_id=blk_dev(offset), device_id_type=MESH)
    for offset in range(1, n_grp):
        pl.semaphore_signal(barrier, inc=1, device_id=grp_dev(offset), device_id_type=MESH)

    sub = iota((8, 128), 0)
    id0 = ids_ref[0]
    id1 = ids_ref[1]
    id_send[...] = jnp.where((sub & 2) == 0, id0, id1)
    own_row, own_col = split_grid(jnp.where((sub & 1) == 0, id0, id1))

    pl.semaphore_wait(barrier, len(offsets) + n_grp - 1)

    id_copies = []
    for s in range(STEPS):
        copy = pltpu.make_async_remote_copy(
            id_send, id_recv.at[s], id_ss.at[s], id_rs.at[s],
            device_id=blk_dev(s + 1), device_id_type=MESH,
        )
        copy.start()
        id_copies.append(copy)
    band_copies = []
    for s in range(STEPS):
        copy = pltpu.make_async_remote_copy(
            band_hbm, band_recv.at[s], b_ss.at[s], b_rs.at[s],
            device_id=blk_dev(s + 1), device_id_type=MESH,
        )
        copy.start()
        band_copies.append(copy)

    col = iota((PAIRS * 16, 256), 0) & 15
    lane = iota((PAIRS * 16, 256), 1)
    shuffle_d[...] = jnp.where(col == (lane >> 6) * 4 + ((lane >> 2) & 3), 1.0, 0.0).astype(BF16)
    shuffle_e[...] = jnp.where(col[:128] == (lane[:128] & 15), 1.0, 0.0).astype(BF16)
    shuffle_m[...] = jnp.where(
        iota((256, 256), 0) == ((lane & 15) << 4) + (lane >> 4), 1.0, 0.0
    ).astype(BF16)

    for copy in id_copies:
        copy.wait_recv()
    class_tiles = []
    for t in range(2):
        other = jnp.where(sub < 4, id_recv[2 * t], id_recv[2 * t + 1])
        row, column = split_grid(other)
        d_row = own_row - row
        d_col = own_col - column
        momentum = jnp.where(d_row < 0, d_row + NKX, d_row) * NKY + jnp.where(
            d_col < 0, d_col + NKY, d_col
        )
        q_slots[0, 8 * t : 8 * t + 8] = momentum
        class_tiles.append(
            jnp.where(d_row < 0, 1, 0) + jnp.where(d_col < 0, 2, 0)
        )
    q_copies = []
    for t in range(1, n_grp):
        copy = pltpu.make_async_remote_copy(
            q_slots.at[0], q_slots.at[t], q_ss.at[t], q_rs.at[t],
            device_id=grp_dev(t), device_id_type=MESH,
        )
        copy.start()
        q_copies.append(copy)

    locals_[0].wait()

    def tiles_of(states):
        x = states.astype(F32)
        y = pltpu.roll(x, 4, 0)
        low = iota(x.shape, 0) < 4
        return jnp.where(low, x, y), jnp.where(low, y, x)

    def repeated(states, first):
        x = states.astype(F32)
        low = iota(x.shape, 0) < 4
        return [
            jnp.where(low, x[first + 2 * h : first + 2 * h + 1], x[first + 2 * h + 1 : first + 2 * h + 2])
            for h in range(2)
        ]

    def store_products(row, rep, tiled):
        products[row : row + 16] = jnp.concatenate(
            [(rep[0] * tiled), (rep[1] * tiled)], axis=0
        ).astype(BF16)

    n_rho = PAIRS * 16
    pair_row = 2 * n_rho
    own_row0 = pair_row + STEPS * KD * 16
    own = [band[i] for i in range(KD)]
    for i in range(KD):
        _, tiled_c = tiles_of(own[i])
        store_products(own_row0 + 16 * i, repeated(own[i], 0), tiled_c)

    for copy in q_copies:
        copy.wait_recv()
    locals_[1].wait()
    wanted = q_slots[...].reshape(n_grp * 16, 128)[:, :1] - grp * owned
    one_hot = jnp.where(
        jnp.broadcast_to(wanted, (n_grp * 16, owned)) == iota((n_grp * 16, owned), 1), 1.0, 0.0
    ).astype(BF16)
    w_send[...] = dot_nn(one_hot, screened[...]).astype(BF16).reshape(n_grp, 16, points)
    w_copies = []
    for t in range(1, n_grp):
        copy = pltpu.make_async_remote_copy(
            w_send.at[t], w_recv.at[t], w_ss.at[t], w_rs.at[t],
            device_id=grp_dev(-t), device_id_type=MESH,
        )
        copy.start()
        w_copies.append(copy)

    for s in range(STEPS):
        band_copies[s].wait_recv()
        for j in range(KD):
            other = band_recv[s, j]
            tiled_v, tiled_c = tiles_of(other)
            store_products(pair_row + (s * KD + j) * 16, repeated(other, 0), tiled_c)
            for i in range(KD):
                p = (s * KD + j) * KD + i
                store_products(p * 16, repeated(own[i], NV), tiled_c)
                store_products(n_rho + p * 16, repeated(own[i], 0), tiled_v)

    locals_[2].wait()
    densities[...] = dot_nn(products[...], planes[...]).astype(BF16)

    locals_[4].wait()
    own_x = (densities[own_row0 : own_row0 + 32].astype(F32) * coulomb[...]).astype(BF16)
    exchange = dot_nt(own_x, densities[pair_row : pair_row + STEPS * KD * 16])
    spread = jnp.concatenate([exchange] * (STEPS * KD), axis=0)
    spread = jnp.where(
        (iota(spread.shape, 0) >> 5) == (iota(spread.shape, 1) >> 4), spread, 0.0
    )
    spread_x = split_dot(spread, shuffle_e[...])
    mrow = iota((n_rho, 256), 0) & 15
    mlane = iota((n_rho, 256), 1)
    total_x = jnp.where(mrow == (mlane >> 4), 2.0 * spread_x, 0.0)

    locals_[3].wait()
    for copy in w_copies:
        copy.wait_recv()
    for t in range(2):
        rows = pl.ds(8 * t, 8)
        got = w_send[0].astype(F32)[8 * t : 8 * t + 8]
        for g in range(1, n_grp):
            got = got + w_recv[g].astype(F32)[8 * t : 8 * t + 8]
        shift = class_tiles[t]
        for o in range(points // 128):
            lanes = slice(o * 128, o * 128 + 128)
            index = jnp.where(
                shift < 2,
                jnp.where(shift == 0, umklapp[0:1, lanes], umklapp[1:2, lanes]),
                jnp.where(shift == 2, umklapp[2:3, lanes], umklapp[3:4, lanes]),
            )
            inner = index & 127
            outer = index >> 7
            acc = jnp.zeros((8, 128), F32)
            for c in range(points // 128):
                part = jnp.take_along_axis(
                    got[:, c * 128 : c * 128 + 128], inner, axis=1, mode="promise_in_bounds"
                )
                acc = jnp.where(outer == c, part, acc)
            screen[rows, lanes] = acc

    for p in range(PAIRS):
        weighted[p * 16 : p * 16 + 16] = (
            densities[p * 16 : p * 16 + 16].astype(F32) * screen[p : p + 1]
        ).astype(BF16)
    direct = dot_nt(weighted[...], densities[n_rho : 2 * n_rho])
    direct = jnp.where((iota(direct.shape, 0) >> 4) == (iota(direct.shape, 1) >> 4), direct, 0.0)
    spread_d = split_dot(direct, shuffle_d[...])
    total = total_x - jnp.where(
        mrow == ((mlane >> 4) & 3) * 4 + (mlane & 3), spread_d, 0.0
    )
    total = total.reshape(PAIRS, 16, 256).sum(axis=1) * (1.0 / math.sqrt(points))
    turned = split_dot(total, shuffle_m[...])

    m_copies = []
    for s in range(STEPS):
        for j in range(KD):
            for i in range(KD):
                p = (s * KD + j) * KD + i
                m_send[s, j : j + 1, i * 256 : i * 256 + 256] = turned[p : p + 1]
        copy = pltpu.make_async_remote_copy(
            m_send.at[s], m_recv.at[s], m_ss.at[s], m_rs.at[s],
            device_id=blk_dev(-(s + 1)), device_id_type=MESH,
        )
        copy.start()
        m_copies.append(copy)
    for s in range(STEPS):
        for j in range(KD):
            for i in range(KD):
                p = (s * KD + j) * KD + i
                out_ref[i, s : s + 1, j * 256 : j * 256 + 256] = total[p : p + 1]
    for copy in id_copies + q_copies + w_copies + band_copies:
        copy.wait_send()
    for s in range(STEPS):
        m_copies[s].wait_recv()
        for k in range(KD):
            mirror_ref[k, s : s + 1] = m_recv[s, k : k + 1]
    for copy in m_copies:
        copy.wait_send()


def per_device(n_grp, n_blk, band_states, kpoint_ids, screened, coulomb, umklapp_map):
    points = band_states.shape[2]
    owned = screened.shape[0]
    rows = 2 * PAIRS * 16 + STEPS * KD * 16 + KD * 16
    planes = jnp.asarray(plane_table(points))
    any_spec = pl.BlockSpec(memory_space=pl.ANY)
    dma = pltpu.SemaphoreType.DMA
    shape = jax.ShapeDtypeStruct((KD, STEPS, KD * 256), F32)
    return pl.pallas_call(
        functools.partial(kernel_body, n_grp, n_blk),
        out_shape=(shape, shape),
        in_specs=[pl.BlockSpec(memory_space=pltpu.SMEM)] + [any_spec] * 5,
        out_specs=(pl.BlockSpec(memory_space=pltpu.VMEM),) * 2,
        scratch_shapes=[
            pltpu.VMEM((KD, NB, points), BF16),
            pltpu.VMEM((owned, points), BF16),
            pltpu.VMEM((1, points), F32),
            pltpu.VMEM((4, points), I32),
            pltpu.VMEM((points, points), BF16),
            pltpu.VMEM((8, 128), I32),
            pltpu.VMEM((STEPS, 8, 128), I32),
            pltpu.VMEM((n_grp, 16, 128), I32),
            pltpu.VMEM((n_grp, 16, points), BF16),
            pltpu.VMEM((n_grp, 16, points), BF16),
            pltpu.VMEM((STEPS, KD, NB, points), BF16),
            pltpu.VMEM((rows, points), BF16),
            pltpu.VMEM((rows, points), BF16),
            pltpu.VMEM((PAIRS * 16, points), BF16),
            pltpu.VMEM((16, points), F32),
            pltpu.VMEM((256, 256), BF16),
            pltpu.VMEM((128, 256), BF16),
            pltpu.VMEM((256, 256), BF16),
            pltpu.VMEM((STEPS, KD, 512), F32),
            pltpu.VMEM((STEPS, KD, 512), F32),
            dma((5,)),
            dma((STEPS,)), dma((STEPS,)),
            dma((n_grp,)), dma((n_grp,)),
            dma((n_grp,)), dma((n_grp,)),
            dma((STEPS,)), dma((STEPS,)),
            dma((STEPS,)), dma((STEPS,)),
        ],
        compiler_params=pltpu.CompilerParams(
            collective_id=0, has_side_effects=True, vmem_limit_bytes=40 * 2**20
        ),
    )(kpoint_ids, band_states, screened, coulomb.reshape(1, points), umklapp_map, planes)


def solution(mesh):
    return jax.shard_map(
        functools.partial(per_device, mesh.shape["grp"], mesh.shape["blk"]),
        mesh=mesh,
        in_specs=(P(("grp", "blk"), None, None), P(("grp", "blk")), P("grp", None), P(), P()),
        out_specs=(P(("grp", "blk"), None, None), P(("grp", "blk"), None, None)),
        check_vma=False,
    )
```

```python
import functools
import math

import jax
import jax.numpy as jnp
import ml_dtypes
import numpy as np
from jax import lax
from jax.experimental import pallas as pl
from jax.experimental.pallas import tpu as pltpu
from jax.sharding import PartitionSpec as P

NKX = 48
NKY = 48
NV = 4
NC = 4
STEPS = 4
KD = 2
NB = NV + NC
PAIRS = STEPS * KD * KD
MESH = pl.DeviceIdType.MESH
F32 = jnp.float32
BF16 = jnp.bfloat16
I32 = jnp.int32


def plane_table(points):
    indices = np.arange(points, dtype=np.int64)
    phase_index = (2 * indices[:, None] + 1) * (2 * indices[None, :] + 1) % (8 * points)
    angles = phase_index * (math.pi / (4 * points))
    return (np.cos(angles) * math.sqrt(2.0 / points)).astype(np.float32).astype(ml_dtypes.bfloat16)


def dot_nn(a, b):
    return lax.dot_general(a, b, (((1,), (0,)), ((), ())), preferred_element_type=F32)


def dot_nt(a, b):
    return lax.dot_general(a, b, (((1,), (1,)), ((), ())), preferred_element_type=F32)


def iota(shape, dim):
    return lax.broadcasted_iota(I32, shape, dim)


def split_dot(value, table):
    rows = value.shape[0]
    high = value.astype(BF16)
    low = (value - high.astype(F32)).astype(BF16)
    both = dot_nn(jnp.concatenate([high, low], axis=0), table)
    return both[:rows] + both[rows:]


def split_grid(ids):
    row = (ids * 43691) >> 21
    return row, ids - row * NKY


def kernel_body(
    n_grp, n_blk, ids_ref, band_hbm, screened_hbm, coulomb_hbm, umklapp_hbm, planes_hbm,
    out_ref, mirror_ref,
    band, screened, coulomb, umklapp, planes,
    id_send, id_recv, q_slots, w_send, w_recv, band_recv,
    products, densities, weighted, screen, shuffle_d, shuffle_e, shuffle_m, m_send, rows_out,
    local_sem, id_ss, id_rs, q_ss, q_rs, w_ss, w_rs, b_ss, b_rs, m_ss, m_rs,
):
    grp = lax.axis_index("grp")
    blk = lax.axis_index("blk")
    points = planes.shape[1]
    owned = screened.shape[0]

    locals_ = [
        pltpu.make_async_copy(src, dst, local_sem.at[n])
        for n, (src, dst) in enumerate(
            [
                (band_hbm, band),
                (screened_hbm, screened),
                (planes_hbm, planes),
                (umklapp_hbm, umklapp),
                (coulomb_hbm, coulomb),
            ]
        )
    ]
    for copy in locals_:
        copy.start()

    def blk_dev(offset):
        return (grp, lax.rem(blk + offset + n_blk, n_blk))

    def grp_dev(offset):
        return (lax.rem(grp + offset + n_grp, n_grp), blk)

    barrier = pltpu.get_barrier_semaphore()
    offsets = sorted({s % n_blk for s in range(1, STEPS + 1)} | {-s % n_blk for s in range(1, STEPS + 1)})
    for offset in offsets:
        pl.semaphore_signal(barrier, inc=1, device_id=blk_dev(offset), device_id_type=MESH)
    for offset in range(1, n_grp):
        pl.semaphore_signal(barrier, inc=1, device_id=grp_dev(offset), device_id_type=MESH)

    sub = iota((8, 128), 0)
    id0 = ids_ref[0]
    id1 = ids_ref[1]
    id_send[...] = jnp.where((sub & 2) == 0, id0, id1)
    own_row, own_col = split_grid(jnp.where((sub & 1) == 0, id0, id1))

    pl.semaphore_wait(barrier, len(offsets) + n_grp - 1)

    id_copies = []
    for s in range(STEPS):
        copy = pltpu.make_async_remote_copy(
            id_send, id_recv.at[s], id_ss.at[s], id_rs.at[s],
            device_id=blk_dev(s + 1), device_id_type=MESH,
        )
        copy.start()
        id_copies.append(copy)
    col = iota((PAIRS * 16, 256), 0) & 15
    lane = iota((PAIRS * 16, 256), 1)
    shuffle_d[...] = jnp.where(col == (lane >> 6) * 4 + ((lane >> 2) & 3), 1.0, 0.0).astype(BF16)
    shuffle_e[...] = jnp.where(col[:128] == (lane[:128] & 15), 1.0, 0.0).astype(BF16)
    shuffle_m[...] = jnp.where(
        iota((256, 256), 0) == ((lane & 15) << 4) + (lane >> 4), 1.0, 0.0
    ).astype(BF16)

    for copy in id_copies:
        copy.wait_recv()
    class_tiles = []
    for t in range(2):
        other = jnp.where(sub < 4, id_recv[2 * t], id_recv[2 * t + 1])
        row, column = split_grid(other)
        d_row = own_row - row
        d_col = own_col - column
        momentum = jnp.where(d_row < 0, d_row + NKX, d_row) * NKY + jnp.where(
            d_col < 0, d_col + NKY, d_col
        )
        q_slots[0, 8 * t : 8 * t + 8] = momentum
        class_tiles.append(
            jnp.where(d_row < 0, 1, 0) + jnp.where(d_col < 0, 2, 0)
        )
    q_copies = []
    for t in range(1, n_grp):
        copy = pltpu.make_async_remote_copy(
            q_slots.at[0], q_slots.at[t], q_ss.at[t], q_rs.at[t],
            device_id=grp_dev(t), device_id_type=MESH,
        )
        copy.start()
        q_copies.append(copy)

    band_copies = []
    for s in range(STEPS):
        copy = pltpu.make_async_remote_copy(
            band_hbm, band_recv.at[s], b_ss.at[s], b_rs.at[s],
            device_id=blk_dev(s + 1), device_id_type=MESH,
        )
        copy.start()
        band_copies.append(copy)

    locals_[0].wait()

    def tiles_of(states):
        x = states.astype(F32)
        y = pltpu.roll(x, 4, 0)
        low = iota(x.shape, 0) < 4
        return jnp.where(low, x, y), jnp.where(low, y, x)

    def repeated(states, first):
        x = states.astype(F32)
        low = iota(x.shape, 0) < 4
        return [
            jnp.where(low, x[first + 2 * h : first + 2 * h + 1], x[first + 2 * h + 1 : first + 2 * h + 2])
            for h in range(2)
        ]

    def store_products(row, rep, tiled):
        products[row : row + 16] = jnp.concatenate(
            [(rep[0] * tiled), (rep[1] * tiled)], axis=0
        ).astype(BF16)

    n_rho = PAIRS * 16
    pair_row = 2 * n_rho
    own_row0 = pair_row + STEPS * KD * 16
    own = [band[i] for i in range(KD)]
    for i in range(KD):
        _, tiled_c = tiles_of(own[i])
        store_products(own_row0 + 16 * i, repeated(own[i], 0), tiled_c)

    for copy in q_copies:
        copy.wait_recv()
    locals_[1].wait()
    wanted = jnp.concatenate(
        [q_slots[t, 8 * h : 8 * h + 8] for h in range(2) for t in range(n_grp)], axis=0
    )[:, :1] - grp * owned
    one_hot = jnp.where(
        jnp.broadcast_to(wanted, (n_grp * 16, owned)) == iota((n_grp * 16, owned), 1), 1.0, 0.0
    ).astype(BF16)
    w_send[...] = dot_nn(one_hot, screened[...]).reshape(2, n_grp, 8, points).astype(BF16)
    w_copies = [[], []]
    for h in range(2):
        for t in range(1, n_grp):
            copy = pltpu.make_async_remote_copy(
                w_send.at[h, t], w_recv.at[h, t], w_ss.at[h, t], w_rs.at[h, t],
                device_id=grp_dev(-t), device_id_type=MESH,
            )
            copy.start()
            w_copies[h].append(copy)

    for s in range(STEPS):
        band_copies[s].wait_recv()
        for j in range(KD):
            other = band_recv[s, j]
            tiled_v, tiled_c = tiles_of(other)
            store_products(pair_row + (s * KD + j) * 16, repeated(other, 0), tiled_c)
            for i in range(KD):
                p = (s * KD + j) * KD + i
                store_products(p * 16, repeated(own[i], NV), tiled_c)
                store_products(n_rho + p * 16, repeated(own[i], 0), tiled_v)

    locals_[2].wait()
    densities[...] = dot_nn(products[...], planes[...]).astype(BF16)

    locals_[4].wait()
    own_x = (densities[own_row0 : own_row0 + 32].astype(F32) * coulomb[...].reshape(1, points)).astype(BF16)
    exchange = dot_nt(own_x, densities[pair_row : pair_row + STEPS * KD * 16])
    spread = jnp.concatenate([exchange] * (STEPS * KD), axis=0)
    spread = jnp.where(
        (iota(spread.shape, 0) >> 5) == (iota(spread.shape, 1) >> 4), spread, 0.0
    )
    spread_x = split_dot(spread, shuffle_e[...])
    half = n_rho // 2
    mrow = iota((half, 256), 0) & 15
    mlane = iota((half, 256), 1)
    keep_x = mrow == (mlane >> 4)
    keep_d = mrow == ((mlane >> 4) & 3) * 4 + (mlane & 3)
    diagonal = (iota((half, half), 0) >> 4) == (iota((half, half), 1) >> 4)
    total_x = [
        jnp.where(keep_x, 2.0 * spread_x[h * half : h * half + half], 0.0) for h in range(2)
    ]

    locals_[3].wait()
    m_copies = []
    for h in range(2):
        shift = class_tiles[h]
        inner = []
        outer = []
        for o in range(points // 128):
            lanes = slice(o * 128, o * 128 + 128)
            index = jnp.where(
                shift < 2,
                jnp.where(shift == 0, umklapp[0:1, lanes], umklapp[1:2, lanes]),
                jnp.where(shift == 2, umklapp[2:3, lanes], umklapp[3:4, lanes]),
            )
            inner.append(index & 127)
            outer.append(index >> 7)
        for copy in w_copies[h]:
            copy.wait_recv()
        got = w_send[h, 0].astype(F32)
        for g in range(1, n_grp):
            got = got + w_recv[h, g].astype(F32)
        for o in range(points // 128):
            acc = jnp.zeros((8, 128), F32)
            for c in range(points // 128):
                part = jnp.take_along_axis(
                    got[:, c * 128 : c * 128 + 128], inner[o], axis=1, mode="promise_in_bounds"
                )
                acc = jnp.where(outer[o] == c, part, acc)
            screen[8 * h : 8 * h + 8, o * 128 : o * 128 + 128] = acc

        first = h * half
        for p in range(8 * h, 8 * h + 8):
            weighted[p * 16 : p * 16 + 16] = (
                densities[p * 16 : p * 16 + 16].astype(F32) * screen[p : p + 1]
            ).astype(BF16)
        direct = dot_nt(
            weighted[first : first + half], densities[n_rho + first : n_rho + first + half]
        )
        spread_d = split_dot(jnp.where(diagonal, direct, 0.0), shuffle_d[:half])
        total = total_x[h] - jnp.where(keep_d, spread_d, 0.0)
        total = total.reshape(8, 16, 256).sum(axis=1) * (1.0 / math.sqrt(points))
        turned = split_dot(total, shuffle_m[...])
        for s in (2 * h, 2 * h + 1):
            for j in range(KD):
                for i in range(KD):
                    p = (s * KD + j) * KD + i - 8 * h
                    m_send[s, j : j + 1, i * 256 : i * 256 + 256] = turned[p : p + 1]
            copy = pltpu.make_async_remote_copy(
                m_send.at[s], mirror_ref.at[s], m_ss.at[s], m_rs.at[s],
                device_id=blk_dev(-(s + 1)), device_id_type=MESH,
            )
            copy.start()
            m_copies.append(copy)
        for s in (2 * h, 2 * h + 1):
            for j in range(KD):
                for i in range(KD):
                    p = (s * KD + j) * KD + i - 8 * h
                    rows_out[i, s : s + 1, j * 256 : j * 256 + 256] = total[p : p + 1]
    out_copy = pltpu.make_async_copy(rows_out, out_ref, local_sem.at[5])
    out_copy.start()
    for copy in id_copies + q_copies + w_copies[0] + w_copies[1] + band_copies:
        copy.wait_send()
    for copy in m_copies:
        copy.wait_recv()
    out_copy.wait()
    for copy in m_copies:
        copy.wait_send()


def finish_body(blocks, turned, out_ref, mirror_ref):
    out_ref[...] = blocks[...]
    for s in range(STEPS):
        for k in range(KD):
            mirror_ref[k, s : s + 1] = turned[s, k : k + 1]


def per_device(n_grp, n_blk, band_states, kpoint_ids, screened, coulomb, umklapp_map):
    points = band_states.shape[2]
    owned = screened.shape[0]
    rows = 2 * PAIRS * 16 + STEPS * KD * 16 + KD * 16
    planes = jnp.asarray(plane_table(points))
    any_spec = pl.BlockSpec(memory_space=pltpu.HBM)
    dma = pltpu.SemaphoreType.DMA
    shape = jax.ShapeDtypeStruct((KD, STEPS, KD * 256), F32)
    arrived = jax.ShapeDtypeStruct((STEPS, KD, KD * 256), F32)
    blocks, turned = pl.pallas_call(
        functools.partial(kernel_body, n_grp, n_blk),
        out_shape=(shape, arrived),
        in_specs=[pl.BlockSpec(memory_space=pltpu.SMEM)] + [any_spec] * 5,
        out_specs=(any_spec,) * 2,
        scratch_shapes=[
            pltpu.VMEM((KD, NB, points), BF16),
            pltpu.VMEM((owned, points), BF16),
            pltpu.VMEM((points,), F32),
            pltpu.VMEM((4, points), I32),
            pltpu.VMEM((points, points), BF16),
            pltpu.VMEM((8, 128), I32),
            pltpu.VMEM((STEPS, 8, 128), I32),
            pltpu.VMEM((n_grp, 16, 128), I32),
            pltpu.VMEM((2, n_grp, 8, points), BF16),
            pltpu.VMEM((2, n_grp, 8, points), BF16),
            pltpu.VMEM((STEPS, KD, NB, points), BF16),
            pltpu.VMEM((rows, points), BF16),
            pltpu.VMEM((rows, points), BF16),
            pltpu.VMEM((PAIRS * 16, points), BF16),
            pltpu.VMEM((16, points), F32),
            pltpu.VMEM((256, 256), BF16),
            pltpu.VMEM((128, 256), BF16),
            pltpu.VMEM((256, 256), BF16),
            pltpu.VMEM((STEPS, KD, 512), F32),
            pltpu.VMEM((KD, STEPS, 512), F32),
            dma((6,)),
            dma((STEPS,)), dma((STEPS,)),
            dma((n_grp,)), dma((n_grp,)),
            dma((2, n_grp)), dma((2, n_grp)),
            dma((STEPS,)), dma((STEPS,)),
            dma((STEPS,)), dma((STEPS,)),
        ],
        compiler_params=pltpu.CompilerParams(
            collective_id=0, has_side_effects=True, vmem_limit_bytes=63 * 2**20
        ),
    )(kpoint_ids, band_states, screened, coulomb, umklapp_map, planes)
    return pl.pallas_call(
        finish_body,
        out_shape=(shape, shape),
        in_specs=[pl.BlockSpec(memory_space=pltpu.VMEM)] * 2,
        out_specs=(pl.BlockSpec(memory_space=pltpu.VMEM),) * 2,
        compiler_params=pltpu.CompilerParams(vmem_limit_bytes=63 * 2**20),
    )(blocks, turned)


def solution(mesh):
    return jax.shard_map(
        functools.partial(per_device, mesh.shape["grp"], mesh.shape["blk"]),
        mesh=mesh,
        in_specs=(P(("grp", "blk"), None, None), P(("grp", "blk")), P("grp", None), P(), P()),
        out_specs=(P(("grp", "blk"), None, None), P(("grp", "blk"), None, None)),
        check_vma=False,
    )
```

```python
import functools
import math

import jax
import jax.numpy as jnp
import ml_dtypes
import numpy as np
from jax import lax
from jax.experimental import pallas as pl
from jax.experimental.pallas import tpu as pltpu
from jax.sharding import PartitionSpec as P

NKX = 48
NKY = 48
NV = 4
NC = 4
STEPS = 4
KD = 2
NB = NV + NC
PAIRS = STEPS * KD * KD
MESH = pl.DeviceIdType.MESH
F32 = jnp.float32
BF16 = jnp.bfloat16
I32 = jnp.int32


def plane_table(points):
    indices = np.arange(points, dtype=np.int64)
    phase_index = (2 * indices[:, None] + 1) * (2 * indices[None, :] + 1) % (8 * points)
    angles = phase_index * (math.pi / (4 * points))
    return (np.cos(angles) * math.sqrt(2.0 / points)).astype(np.float32).astype(ml_dtypes.bfloat16)


def dot_nn(a, b):
    return lax.dot_general(a, b, (((1,), (0,)), ((), ())), preferred_element_type=F32)


def dot_nt(a, b):
    return lax.dot_general(a, b, (((1,), (1,)), ((), ())), preferred_element_type=F32)


def iota(shape, dim):
    return lax.broadcasted_iota(I32, shape, dim)


def split_dot(value, table):
    rows = value.shape[0]
    high = value.astype(BF16)
    low = (value - high.astype(F32)).astype(BF16)
    both = dot_nn(jnp.concatenate([high, low], axis=0), table)
    return both[:rows] + both[rows:]


def split_grid(ids):
    row = (ids * 43691) >> 21
    return row, ids - row * NKY


def kernel_body(
    n_grp, n_blk, ids_hbm, band_hbm, screened_hbm, coulomb_hbm, umklapp_hbm, planes_hbm,
    out_ref, mirror_ref,
    ids_ref, band, screened, coulomb, umklapp, planes,
    id_send, id_recv, q_slots, w_send, w_recv, band_recv,
    products, densities, weighted, screen, shuffle_d, shuffle_e, shuffle_m, m_send, rows_out,
    local_sem, id_ss, id_rs, q_ss, q_rs, w_ss, w_rs, b_ss, b_rs, m_ss, m_rs,
):
    grp = lax.axis_index("grp")
    blk = lax.axis_index("blk")
    points = planes.shape[1]
    owned = screened.shape[0]

    ids_copy = pltpu.make_async_copy(ids_hbm, ids_ref, local_sem.at[6])
    ids_copy.start()
    locals_ = [
        pltpu.make_async_copy(src, dst, local_sem.at[n])
        for n, (src, dst) in enumerate(
            [
                (band_hbm, band),
                (screened_hbm, screened),
                (planes_hbm, planes),
                (umklapp_hbm, umklapp),
                (coulomb_hbm, coulomb),
            ]
        )
    ]

    def blk_dev(offset):
        return (grp, lax.rem(blk + offset + n_blk, n_blk))

    def grp_dev(offset):
        return (lax.rem(grp + offset + n_grp, n_grp), blk)

    barrier = pltpu.get_barrier_semaphore()
    offsets = sorted({s % n_blk for s in range(1, STEPS + 1)} | {-s % n_blk for s in range(1, STEPS + 1)})
    for offset in offsets:
        pl.semaphore_signal(barrier, inc=1, device_id=blk_dev(offset), device_id_type=MESH)
    for offset in range(1, n_grp):
        pl.semaphore_signal(barrier, inc=1, device_id=grp_dev(offset), device_id_type=MESH)

    for copy in locals_:
        copy.start()
    sub = iota((8, 128), 0)
    ids_copy.wait()
    id0 = ids_ref[0]
    id1 = ids_ref[1]
    id_send[...] = jnp.where((sub & 2) == 0, id0, id1)
    own_row, own_col = split_grid(jnp.where((sub & 1) == 0, id0, id1))

    pl.semaphore_wait(barrier, len(offsets) + n_grp - 1)

    id_copies = []
    for s in range(STEPS):
        copy = pltpu.make_async_remote_copy(
            id_send, id_recv.at[s], id_ss.at[s], id_rs.at[s],
            device_id=blk_dev(s + 1), device_id_type=MESH,
        )
        copy.start()
        id_copies.append(copy)
    col = iota((PAIRS * 16, 256), 0) & 15
    lane = iota((PAIRS * 16, 256), 1)
    shuffle_d[...] = jnp.where(col == (lane >> 6) * 4 + ((lane >> 2) & 3), 1.0, 0.0).astype(BF16)
    shuffle_e[...] = jnp.where(col[:128] == (lane[:128] & 15), 1.0, 0.0).astype(BF16)
    shuffle_m[...] = jnp.where(
        iota((256, 256), 0) == ((lane & 15) << 4) + (lane >> 4), 1.0, 0.0
    ).astype(BF16)

    for copy in id_copies:
        copy.wait_recv()
    class_tiles = []
    for t in range(2):
        other = jnp.where(sub < 4, id_recv[2 * t], id_recv[2 * t + 1])
        row, column = split_grid(other)
        d_row = own_row - row
        d_col = own_col - column
        momentum = jnp.where(d_row < 0, d_row + NKX, d_row) * NKY + jnp.where(
            d_col < 0, d_col + NKY, d_col
        )
        q_slots[0, 8 * t : 8 * t + 8] = momentum
        class_tiles.append(
            jnp.where(d_row < 0, 1, 0) + jnp.where(d_col < 0, 2, 0)
        )
    q_copies = []
    for t in range(1, n_grp):
        copy = pltpu.make_async_remote_copy(
            q_slots.at[0], q_slots.at[t], q_ss.at[t], q_rs.at[t],
            device_id=grp_dev(t), device_id_type=MESH,
        )
        copy.start()
        q_copies.append(copy)

    band_copies = []
    for s in range(STEPS):
        copy = pltpu.make_async_remote_copy(
            band_hbm, band_recv.at[s], b_ss.at[s], b_rs.at[s],
            device_id=blk_dev(s + 1), device_id_type=MESH,
        )
        copy.start()
        band_copies.append(copy)

    locals_[0].wait()

    def tiles_of(states):
        x = states.astype(F32)
        y = pltpu.roll(x, 4, 0)
        low = iota(x.shape, 0) < 4
        return jnp.where(low, x, y), jnp.where(low, y, x)

    def repeated(states, first):
        x = states.astype(F32)
        low = iota(x.shape, 0) < 4
        return [
            jnp.where(low, x[first + 2 * h : first + 2 * h + 1], x[first + 2 * h + 1 : first + 2 * h + 2])
            for h in range(2)
        ]

    def store_products(row, rep, tiled):
        products[row : row + 16] = jnp.concatenate(
            [(rep[0] * tiled), (rep[1] * tiled)], axis=0
        ).astype(BF16)

    n_rho = PAIRS * 16
    pair_row = 2 * n_rho
    own_row0 = pair_row + STEPS * KD * 16
    own = [band[i] for i in range(KD)]
    for i in range(KD):
        _, tiled_c = tiles_of(own[i])
        store_products(own_row0 + 16 * i, repeated(own[i], 0), tiled_c)

    for copy in q_copies:
        copy.wait_recv()
    locals_[1].wait()
    wanted = jnp.concatenate(
        [q_slots[t, 8 * h : 8 * h + 8] for h in range(2) for t in range(n_grp)], axis=0
    )[:, :1] - grp * owned
    one_hot = jnp.where(
        jnp.broadcast_to(wanted, (n_grp * 16, owned)) == iota((n_grp * 16, owned), 1), 1.0, 0.0
    ).astype(BF16)
    w_send[...] = dot_nn(one_hot, screened[...]).reshape(2, n_grp, 8, points).astype(BF16)
    w_copies = [[], []]
    for h in range(2):
        for t in range(1, n_grp):
            copy = pltpu.make_async_remote_copy(
                w_send.at[h, t], w_recv.at[h, t], w_ss.at[h, t], w_rs.at[h, t],
                device_id=grp_dev(-t), device_id_type=MESH,
            )
            copy.start()
            w_copies[h].append(copy)

    for s in range(STEPS):
        band_copies[s].wait_recv()
        for j in range(KD):
            other = band_recv[s, j]
            tiled_v, tiled_c = tiles_of(other)
            store_products(pair_row + (s * KD + j) * 16, repeated(other, 0), tiled_c)
            for i in range(KD):
                p = (s * KD + j) * KD + i
                store_products(p * 16, repeated(own[i], NV), tiled_c)
                store_products(n_rho + p * 16, repeated(own[i], 0), tiled_v)

    locals_[2].wait()
    densities[...] = dot_nn(products[...], planes[...]).astype(BF16)

    locals_[4].wait()
    own_x = (densities[own_row0 : own_row0 + 32].astype(F32) * coulomb[...].reshape(1, points)).astype(BF16)
    exchange = dot_nt(own_x, densities[pair_row : pair_row + STEPS * KD * 16])
    spread = jnp.concatenate([exchange] * (STEPS * KD), axis=0)
    spread = jnp.where(
        (iota(spread.shape, 0) >> 5) == (iota(spread.shape, 1) >> 4), spread, 0.0
    )
    spread_x = split_dot(spread, shuffle_e[...])
    half = n_rho // 2
    mrow = iota((half, 256), 0) & 15
    mlane = iota((half, 256), 1)
    keep_x = mrow == (mlane >> 4)
    keep_d = mrow == ((mlane >> 4) & 3) * 4 + (mlane & 3)
    diagonal = (iota((half, half), 0) >> 4) == (iota((half, half), 1) >> 4)
    total_x = [
        jnp.where(keep_x, 2.0 * spread_x[h * half : h * half + half], 0.0) for h in range(2)
    ]

    locals_[3].wait()
    m_copies = []
    for h in range(2):
        shift = class_tiles[h]
        inner = []
        outer = []
        for o in range(points // 128):
            lanes = slice(o * 128, o * 128 + 128)
            index = jnp.where(
                shift < 2,
                jnp.where(shift == 0, umklapp[0:1, lanes], umklapp[1:2, lanes]),
                jnp.where(shift == 2, umklapp[2:3, lanes], umklapp[3:4, lanes]),
            )
            inner.append(index & 127)
            outer.append(index >> 7)
        for copy in w_copies[h]:
            copy.wait_recv()
        got = w_send[h, 0].astype(F32)
        for g in range(1, n_grp):
            got = got + w_recv[h, g].astype(F32)
        for o in range(points // 128):
            acc = jnp.zeros((8, 128), F32)
            for c in range(points // 128):
                part = jnp.take_along_axis(
                    got[:, c * 128 : c * 128 + 128], inner[o], axis=1, mode="promise_in_bounds"
                )
                acc = jnp.where(outer[o] == c, part, acc)
            screen[8 * h : 8 * h + 8, o * 128 : o * 128 + 128] = acc

        first = h * half
        for p in range(8 * h, 8 * h + 8):
            weighted[p * 16 : p * 16 + 16] = (
                densities[p * 16 : p * 16 + 16].astype(F32) * screen[p : p + 1]
            ).astype(BF16)
        direct = dot_nt(
            weighted[first : first + half], densities[n_rho + first : n_rho + first + half]
        )
        spread_d = split_dot(jnp.where(diagonal, direct, 0.0), shuffle_d[:half])
        total = total_x[h] - jnp.where(keep_d, spread_d, 0.0)
        total = total.reshape(8, 16, 256).sum(axis=1) * (1.0 / math.sqrt(points))
        turned = split_dot(total, shuffle_m[...])
        for s in (2 * h, 2 * h + 1):
            for j in range(KD):
                for i in range(KD):
                    p = (s * KD + j) * KD + i - 8 * h
                    m_send[s, j : j + 1, i * 256 : i * 256 + 256] = turned[p : p + 1]
            copy = pltpu.make_async_remote_copy(
                m_send.at[s], mirror_ref.at[s], m_ss.at[s], m_rs.at[s],
                device_id=blk_dev(-(s + 1)), device_id_type=MESH,
            )
            copy.start()
            m_copies.append(copy)
        for s in (2 * h, 2 * h + 1):
            for j in range(KD):
                for i in range(KD):
                    p = (s * KD + j) * KD + i - 8 * h
                    rows_out[i, s : s + 1, j * 256 : j * 256 + 256] = total[p : p + 1]
    out_copy = pltpu.make_async_copy(rows_out, out_ref, local_sem.at[5])
    out_copy.start()
    for copy in id_copies + q_copies + w_copies[0] + w_copies[1] + band_copies:
        copy.wait_send()
    for copy in m_copies:
        copy.wait_recv()
    out_copy.wait()
    for copy in m_copies:
        copy.wait_send()


def finish_body(blocks, turned, out_ref, mirror_ref):
    out_ref[...] = blocks[...]
    for s in range(STEPS):
        for k in range(KD):
            mirror_ref[k, s : s + 1] = turned[s, k : k + 1]


def per_device(n_grp, n_blk, band_states, kpoint_ids, screened, coulomb, umklapp_map):
    points = band_states.shape[2]
    owned = screened.shape[0]
    rows = 2 * PAIRS * 16 + STEPS * KD * 16 + KD * 16
    planes = jnp.asarray(plane_table(points))
    any_spec = pl.BlockSpec(memory_space=pltpu.HBM)
    dma = pltpu.SemaphoreType.DMA
    shape = jax.ShapeDtypeStruct((KD, STEPS, KD * 256), F32)
    arrived = jax.ShapeDtypeStruct((STEPS, KD, KD * 256), F32)
    blocks, turned = pl.pallas_call(
        functools.partial(kernel_body, n_grp, n_blk),
        out_shape=(shape, arrived),
        in_specs=[any_spec] * 6,
        out_specs=(any_spec,) * 2,
        scratch_shapes=[
            pltpu.SMEM((KD,), I32),
            pltpu.VMEM((KD, NB, points), BF16),
            pltpu.VMEM((owned, points), BF16),
            pltpu.VMEM((points,), F32),
            pltpu.VMEM((4, points), I32),
            pltpu.VMEM((points, points), BF16),
            pltpu.VMEM((8, 128), I32),
            pltpu.VMEM((STEPS, 8, 128), I32),
            pltpu.VMEM((n_grp, 16, 128), I32),
            pltpu.VMEM((2, n_grp, 8, points), BF16),
            pltpu.VMEM((2, n_grp, 8, points), BF16),
            pltpu.VMEM((STEPS, KD, NB, points), BF16),
            pltpu.VMEM((rows, points), BF16),
            pltpu.VMEM((rows, points), BF16),
            pltpu.VMEM((PAIRS * 16, points), BF16),
            pltpu.VMEM((16, points), F32),
            pltpu.VMEM((256, 256), BF16),
            pltpu.VMEM((128, 256), BF16),
            pltpu.VMEM((256, 256), BF16),
            pltpu.VMEM((STEPS, KD, 512), F32),
            pltpu.VMEM((KD, STEPS, 512), F32),
            dma((7,)),
            dma((STEPS,)), dma((STEPS,)),
            dma((n_grp,)), dma((n_grp,)),
            dma((2, n_grp)), dma((2, n_grp)),
            dma((STEPS,)), dma((STEPS,)),
            dma((STEPS,)), dma((STEPS,)),
        ],
        compiler_params=pltpu.CompilerParams(
            collective_id=0, has_side_effects=True, vmem_limit_bytes=63 * 2**20
        ),
    )(kpoint_ids, band_states, screened, coulomb, umklapp_map, planes)
    return pl.pallas_call(
        finish_body,
        out_shape=(shape, shape),
        in_specs=[pl.BlockSpec(memory_space=pltpu.VMEM)] * 2,
        out_specs=(pl.BlockSpec(memory_space=pltpu.VMEM),) * 2,
        compiler_params=pltpu.CompilerParams(vmem_limit_bytes=63 * 2**20),
    )(blocks, turned)


def solution(mesh):
    return jax.shard_map(
        functools.partial(per_device, mesh.shape["grp"], mesh.shape["blk"]),
        mesh=mesh,
        in_specs=(P(("grp", "blk"), None, None), P(("grp", "blk")), P("grp", None), P(), P()),
        out_specs=(P(("grp", "blk"), None, None), P(("grp", "blk"), None, None)),
        check_vma=False,
    )
```
